1024 devices in a mesh: blk: 32 (over z, core), row: 8 (over y), depth: 4 (over x).
Axes of the slice: x: 4, y: 8, z: 16, core: 2. Of those that a mesh axis runs over, the one named last changes fastest.
Arguments:
- x_start: bfloat16 [4096, 4096], P('blk', ('row', 'depth')), as said below
- keep_mask: int32 [2, 2, 64, 64], P(None, None, 'blk', ('row', 'depth')), may hold values from 0 to 1, as said below
Outputs:
- sign_estimate: bfloat16 [4096, 4096], P('blk', ('row', 'depth'))
The draws below stay inside these ranges and needn't reach their ends.
Inputs may be any that keep to these rules, and one draw needn't show every extreme that they name: Each pattern is symmetric (keep_mask[t, s, i, j] = keep_mask[t, s, j, i]) and keeps every diagonal block. x_start is exactly symmetric.
All inputs are finite; a program needn't handle non-finite values.
Results may differ from the reference program's by a relative error of at most 0.0036.
Values may be sent and summed in bfloat16 or wider, within the bound.
No kernel may reach another device: no remote copies, remote signals or barrier semaphores. Data moves between devices by JAX's collectives and lax.ppermute only.
A program may use at most 32 MiB of HBM per device.

```python
import math
import jax
import jax.numpy as jnp

BS = 64
ITERS = 2
NB = 64
ORDER = 4096


def spatial_places(key):
    return jax.random.permutation(jax.random.fold_in(key, 101), NB)


def local_pattern(places, key, reach_blocks):
    gap = jnp.abs(places[:, None] - places[None, :])
    gap = jnp.minimum(gap, NB - gap)
    thinned = jax.random.randint(key, (NB, NB), 0, 5) < 4
    rows_idx = jnp.arange(NB)[:, None]
    cols_idx = jnp.arange(NB)[None, :]
    mirrored = jnp.where(rows_idx <= cols_idx, thinned, thinned.T)
    kept = jnp.logical_and(gap <= reach_blocks, mirrored)
    return jnp.where(rows_idx == cols_idx, 1, kept.astype(jnp.int32)).astype(jnp.int32)


def draw_x_start(key, part):
    places = spatial_places(key)
    key = jax.random.fold_in(key, 1)
    key_noise, key_size, key_sign, key_thin = jax.random.split(key, 4)
    reach_blocks = max(1, NB // 8)
    share = (2 * reach_blocks + 1) * 0.8 / NB
    noise = jax.random.normal(key_noise, (ORDER, ORDER), jnp.float32)
    symmetric = (noise + noise.T) * (0.4 / math.sqrt(2.0 * ORDER * share))
    pattern = local_pattern(places, key_thin, reach_blocks)
    element_keep = jnp.repeat(jnp.repeat(pattern, BS, axis=0), BS, axis=1)
    magnitude = jax.random.uniform(key_size, (ORDER,), jnp.float32, 0.4, 0.8)
    signs = jnp.where(jax.random.randint(key_sign, (ORDER,), 0, 2) == 0, -1.0, 1.0).astype(jnp.float32)
    rows_idx = jnp.arange(ORDER)[:, None]
    cols_idx = jnp.arange(ORDER)[None, :]
    diagonal_part = jnp.where(rows_idx == cols_idx, (magnitude * signs)[:, None], jnp.float32(0.0))
    result = jnp.where(element_keep == 1, symmetric, jnp.float32(0.0)) + diagonal_part
    return result.astype(jnp.bfloat16)


def draw_keep_mask(key, part):
    places = spatial_places(key)
    key = jax.random.fold_in(key, 2)
    reach_blocks = max(1, NB // 8)
    layers = []
    for step_index in range(ITERS):
        wide = local_pattern(places, jax.random.fold_in(key, 10 * step_index + 1), 2 * reach_blocks)
        narrow = local_pattern(places, jax.random.fold_in(key, 10 * step_index + 2), reach_blocks)
        layers.append(jnp.stack([wide, narrow]))
    return jnp.stack(layers).astype(jnp.int32)


def setup_inputs(seed: int = 0) -> dict:
    streams_of = jax.random.split(jax.random.key(seed), 3)
    x_start = draw_x_start(jax.random.fold_in(streams_of[2], 71), 0)
    keep_mask = draw_keep_mask(jax.random.fold_in(streams_of[2], 71), 0)
    return dict(x_start=x_start, keep_mask=keep_mask)


def expand_blocks(pattern):
    return jnp.repeat(jnp.repeat(pattern, BS, axis=0), BS, axis=1)


def reference(x_start, keep_mask):
    current = x_start
    for step_index in range(ITERS):
        product = jnp.dot(current, current, preferred_element_type=jnp.float32)
        square = jnp.where(expand_blocks(keep_mask[step_index, 0]) == 1, product, jnp.float32(0.0)).astype(jnp.bfloat16)
        cube_term = jnp.dot(current, square, preferred_element_type=jnp.float32)
        update = 1.5 * current.astype(jnp.float32) - 0.5 * cube_term
        current = jnp.where(expand_blocks(keep_mask[step_index, 1]) == 1, update, jnp.float32(0.0)).astype(jnp.bfloat16)
    return current
```

```python
import functools

import jax
import jax.numpy as jnp
from jax import lax
from jax.experimental import pallas as pl
from jax.experimental.pallas import tpu as pltpu
from jax.sharding import Mesh, PartitionSpec as P

BS = 64
ITERS = 2
CORES = 2
LINE = ("z",)
PLANE = ("row", "depth")
ALL = ("z", "core", "row", "depth")
F32 = jnp.float32
BF16 = jnp.bfloat16


def filtered(value, mask_ref):
    block_row = lax.broadcasted_iota(jnp.int32, value.shape, 0) // BS
    block_col = lax.broadcasted_iota(jnp.int32, value.shape, 1) // BS
    keep = jnp.zeros(value.shape, jnp.int32)
    for i in range(value.shape[0] // BS):
        for j in range(value.shape[1] // BS):
            here = jnp.logical_and(block_row == i, block_col == j)
            keep = jnp.where(here, mask_ref[i, j], keep)
    return jnp.where(keep == 1, value, 0.0).astype(BF16)


def slab_product(core_ref, rows_ref, own_ref, other_ref):
    chips, side, cols = own_ref.shape
    core = core_ref[0]
    total = None
    for col_ref, which in ((own_ref, core), (other_ref, 1 - core)):
        left = jnp.concatenate([rows_ref[2 * z + which] for z in range(chips)], axis=1)
        right = col_ref[...].reshape(chips * side, cols)
        term = jnp.dot(left, right, preferred_element_type=F32)
        total = term if total is None else total + term
    return total


def square_kernel(core_ref, mask_ref, rows_ref, own_ref, other_ref, copies_ref):
    tile = filtered(slab_product(core_ref, rows_ref, own_ref, other_ref), mask_ref)
    for i in range(copies_ref.shape[0]):
        copies_ref[i] = tile


def updated(core_ref, mask_ref, rows_ref, own_ref, other_ref, tile_ref):
    cube_term = slab_product(core_ref, rows_ref, own_ref, other_ref)
    return filtered(1.5 * tile_ref[...].astype(F32) - 0.5 * cube_term, mask_ref)


def update_kernel(core_ref, mask_ref, rows_ref, own_ref, other_ref, tile_ref, out_ref, copies_ref):
    tile = updated(core_ref, mask_ref, rows_ref, own_ref, other_ref, tile_ref)
    out_ref[...] = tile
    for i in range(copies_ref.shape[0]):
        copies_ref[i] = tile


def last_kernel(core_ref, mask_ref, rows_ref, own_ref, other_ref, tile_ref, out_ref):
    tile = updated(core_ref, mask_ref, rows_ref, own_ref, other_ref, tile_ref)
    out_ref[...] = tile.astype(F32).T.astype(BF16)


def call(kernel, scalars, arrays, outs):
    smem = pl.BlockSpec(memory_space=pltpu.SMEM)
    vmem = pl.BlockSpec(memory_space=pltpu.VMEM)
    return pl.pallas_call(
        kernel,
        out_shape=[jax.ShapeDtypeStruct(shape, BF16) for shape in outs],
        in_specs=[smem] * len(scalars) + [vmem] * len(arrays),
        out_specs=[vmem] * len(outs),
        compiler_params=pltpu.CompilerParams(vmem_limit_bytes=32 << 20),
    )(*scalars, *arrays)


def on_device(x_start, keep_mask):
    side = x_start.shape[0]
    tiles = lax.axis_size(PLANE)
    blk = lax.axis_size(LINE) * CORES
    core = lax.axis_index("core").astype(jnp.int32).reshape(1)
    tile, copies = x_start, jnp.broadcast_to(x_start[None], (tiles, side, side))
    for step in range(ITERS):
        rows = lax.all_to_all(copies, PLANE, 0, 0)
        own = lax.all_gather(tile, LINE, axis=0)
        other = lax.ppermute(own, "core", [(0, 1), (1, 0)])
        (copies,) = call(
            square_kernel, [core, keep_mask[step, 0]], [rows, own, other], [(tiles, side, side)]
        )
        rows = lax.all_to_all(copies, PLANE, 0, 0)
        scalars, arrays = [core, keep_mask[step, 1]], [rows, own, other, tile]
        if step < ITERS - 1:
            tile, copies = call(
                update_kernel, scalars, arrays, [(side, side), (tiles, side, side)]
            )
        else:
            (tile,) = call(last_kernel, scalars, arrays, [(side, side)])
    swap = [(b * tiles + c, c * tiles + b) for b in range(blk) for c in range(tiles)]
    return lax.ppermute(tile, ALL, swap)


def solution(mesh):
    blk, row, depth = mesh.devices.shape
    fine = Mesh(mesh.devices.reshape(blk // CORES, CORES, row, depth), ALL)
    spec = P(("z", "core"), PLANE)
    return jax.shard_map(
        on_device,
        mesh=fine,
        in_specs=(spec, P(None, None, ("z", "core"), PLANE)),
        out_specs=spec,
        check_vma=False,
    )
```

```python
import jax
import jax.numpy as jnp
from jax import lax
from jax.experimental import pallas as pl
from jax.experimental.pallas import tpu as pltpu
from jax.sharding import Mesh, PartitionSpec as P

BS = 64
ITERS = 2
CORES = 2
LINE = ("z",)
PLANE = ("row", "depth")
ALL = ("z", "core", "row", "depth")
F32 = jnp.float32
BF16 = jnp.bfloat16


def filtered(value, mask_ref):
    block_row = lax.broadcasted_iota(jnp.int32, value.shape, 0) // BS
    block_col = lax.broadcasted_iota(jnp.int32, value.shape, 1) // BS
    keep = jnp.zeros(value.shape, jnp.int32)
    for i in range(value.shape[0] // BS):
        for j in range(value.shape[1] // BS):
            here = jnp.logical_and(block_row == i, block_col == j)
            keep = jnp.where(here, mask_ref[i, j], keep)
    return jnp.where(keep == 1, value, 0.0).astype(BF16)


def slab_product(core_ref, rows_ref, own_ref, other_ref):
    chips, side, cols = own_ref.shape
    core = core_ref[0]
    total = None
    for col_ref, which in ((own_ref, core), (other_ref, 1 - core)):
        left = jnp.concatenate([rows_ref[2 * z + which] for z in range(chips)], axis=1)
        right = col_ref[...].reshape(chips * side, cols)
        term = jnp.dot(left, right, preferred_element_type=F32)
        total = term if total is None else total + term
    return total


def square_kernel(core_ref, mask_ref, rows_ref, own_ref, other_ref, out_ref):
    out_ref[...] = filtered(slab_product(core_ref, rows_ref, own_ref, other_ref), mask_ref)


def update_kernel(core_ref, mask_ref, rows_ref, own_ref, other_ref, tile_ref, out_ref, *copies_refs):
    cube_term = slab_product(core_ref, rows_ref, own_ref, other_ref)
    tile = filtered(1.5 * tile_ref[...].astype(F32) - 0.5 * cube_term, mask_ref)
    out_ref[...] = tile
    for copies_ref in copies_refs:
        for i in range(copies_ref.shape[0]):
            copies_ref[i] = tile


def call(kernel, scalars, arrays, outs):
    smem = pl.BlockSpec(memory_space=pltpu.SMEM)
    vmem = pl.BlockSpec(memory_space=pltpu.VMEM)
    return pl.pallas_call(
        kernel,
        out_shape=[jax.ShapeDtypeStruct(shape, BF16) for shape in outs],
        in_specs=[smem] * len(scalars) + [vmem] * len(arrays),
        out_specs=[vmem] * len(outs),
        compiler_params=pltpu.CompilerParams(vmem_limit_bytes=32 << 20),
    )(*scalars, *arrays)


def column_slab(tile):
    own = lax.all_gather(tile, LINE, axis=0)
    return own, lax.ppermute(own, "core", [(0, 1), (1, 0)])


def on_device(x_start, keep_mask):
    side = x_start.shape[0]
    tiles = lax.axis_size(PLANE)
    core = lax.axis_index("core").astype(jnp.int32).reshape(1)
    tile, copies = x_start, jnp.broadcast_to(x_start[None], (tiles, side, side))
    for step in range(ITERS):
        rows = lax.all_to_all(copies, PLANE, 0, 0)
        (square,) = call(
            square_kernel, [core, keep_mask[step, 0]], [rows, *column_slab(tile)], [(side, side)]
        )
        outs = [(side, side)] + [(tiles, side, side)] * (step < ITERS - 1)
        tile, *copies = call(
            update_kernel, [core, keep_mask[step, 1]], [rows, *column_slab(square), tile], outs
        )
        copies = copies[0] if copies else None
    return tile


def solution(mesh):
    blk, row, depth = mesh.devices.shape
    fine = Mesh(mesh.devices.reshape(blk // CORES, CORES, row, depth), ALL)
    spec = P(("z", "core"), PLANE)
    return jax.shard_map(
        on_device,
        mesh=fine,
        in_specs=(spec, P(None, None, ("z", "core"), PLANE)),
        out_specs=spec,
        check_vma=False,
    )
```

```python
import jax
import jax.numpy as jnp
from jax import lax
from jax.experimental import pallas as pl
from jax.experimental.pallas import tpu as pltpu
from jax.sharding import PartitionSpec as P

BS = 64
ITERS = 2
CORES = 2
PLANE = ("row", "depth")
F32 = jnp.float32
BF16 = jnp.bfloat16


def filtered(value, mask_ref):
    block_row = lax.broadcasted_iota(jnp.int32, value.shape, 0) // BS
    block_col = lax.broadcasted_iota(jnp.int32, value.shape, 1) // BS
    keep = jnp.zeros(value.shape, jnp.int32)
    for i in range(value.shape[0] // BS):
        for j in range(value.shape[1] // BS):
            here = jnp.logical_and(block_row == i, block_col == j)
            keep = jnp.where(here, mask_ref[i, j], keep)
    return jnp.where(keep == 1, value, 0.0).astype(BF16)


def slab_product(ring_ref, rows_ref, own_ref, other_ref):
    chips, side, cols = own_ref.shape
    total = None
    for col_ref, ring in ((own_ref, ring_ref[0]), (other_ref, 1 - ring_ref[0])):
        cores = [1 - ring if z % 2 else ring for z in range(chips)]
        left = jnp.concatenate([rows_ref[CORES * z + cores[z]] for z in range(chips)], axis=1)
        right = col_ref[...].reshape(chips * side, cols)
        term = jnp.dot(left, right, preferred_element_type=F32)
        total = term if total is None else total + term
    return total


def square_kernel(ring_ref, mask_ref, rows_ref, own_ref, other_ref, out_ref):
    out_ref[...] = filtered(slab_product(ring_ref, rows_ref, own_ref, other_ref), mask_ref)


def update_kernel(ring_ref, mask_ref, rows_ref, own_ref, other_ref, tile_ref, out_ref, *copies_refs):
    cube_term = slab_product(ring_ref, rows_ref, own_ref, other_ref)
    tile = filtered(1.5 * tile_ref[...].astype(F32) - 0.5 * cube_term, mask_ref)
    out_ref[...] = tile
    for copies_ref in copies_refs:
        for i in range(copies_ref.shape[0]):
            copies_ref[i] = tile


def call(kernel, scalars, arrays, outs):
    smem = pl.BlockSpec(memory_space=pltpu.SMEM)
    vmem = pl.BlockSpec(memory_space=pltpu.VMEM)
    return pl.pallas_call(
        kernel,
        out_shape=[jax.ShapeDtypeStruct(shape, BF16) for shape in outs],
        in_specs=[smem] * len(scalars) + [vmem] * len(arrays),
        out_specs=[vmem] * len(outs),
        compiler_params=pltpu.CompilerParams(vmem_limit_bytes=32 << 20),
    )(*scalars, *arrays)


def column_slab(tile):
    chips = lax.axis_size("blk") // CORES
    rings = [[CORES * z + (z + p) % CORES for z in range(chips)] for p in range(CORES)]
    own = lax.all_gather(tile, "blk", axis=0, axis_index_groups=rings)
    swap = [(CORES * z + k, CORES * z + 1 - k) for z in range(chips) for k in range(CORES)]
    return own, lax.ppermute(own, "blk", swap)


def on_device(x_start, keep_mask):
    side = x_start.shape[0]
    tiles = lax.axis_size(PLANE)
    place = lax.axis_index("blk")
    ring = ((place // CORES + place) % CORES).astype(jnp.int32).reshape(1)
    tile, copies = x_start, jnp.broadcast_to(x_start[None], (tiles, side, side))
    for step in range(ITERS):
        rows = lax.all_to_all(copies, PLANE, 0, 0)
        (square,) = call(
            square_kernel, [ring, keep_mask[step, 0]], [rows, *column_slab(tile)], [(side, side)]
        )
        outs = [(side, side)] + [(tiles, side, side)] * (step < ITERS - 1)
        tile, *copies = call(
            update_kernel, [ring, keep_mask[step, 1]], [rows, *column_slab(square), tile], outs
        )
        copies = copies[0] if copies else None
    return tile


def solution(mesh):
    spec = P("blk", PLANE)
    return jax.shard_map(
        on_device,
        mesh=mesh,
        in_specs=(spec, P(None, None, "blk", PLANE)),
        out_specs=spec,
        check_vma=False,
    )
```

```python
import jax
import jax.numpy as jnp
from jax import lax
from jax.experimental import pallas as pl
from jax.experimental.pallas import tpu as pltpu
from jax.sharding import PartitionSpec as P

BS = 64
ITERS = 2
CORES = 2
PLANE = ("row", "depth")
F32 = jnp.float32
BF16 = jnp.bfloat16


def filtered(value, mask_ref):
    block_row = lax.broadcasted_iota(jnp.int32, value.shape, 0) // BS
    block_col = lax.broadcasted_iota(jnp.int32, value.shape, 1) // BS
    keep = jnp.zeros(value.shape, jnp.int32)
    for i in range(value.shape[0] // BS):
        for j in range(value.shape[1] // BS):
            here = jnp.logical_and(block_row == i, block_col == j)
            keep = jnp.where(here, mask_ref[i, j], keep)
    return jnp.where(keep == 1, value, 0.0).astype(BF16)


def ring_product(ring, rows_ref, col_ref):
    chips, side, cols = col_ref.shape
    cores = [1 - ring if z % 2 else ring for z in range(chips)]
    left = jnp.concatenate([rows_ref[CORES * z + cores[z]] for z in range(chips)], axis=1)
    return jnp.dot(left, col_ref[...].reshape(chips * side, cols), preferred_element_type=F32)


def own_kernel(ring_ref, rows_ref, own_ref, out_ref):
    out_ref[...] = ring_product(ring_ref[0], rows_ref, own_ref)


def square_kernel(ring_ref, mask_ref, rows_ref, own_ref, other_ref, out_ref):
    total = own_ref[...] + ring_product(1 - ring_ref[0], rows_ref, other_ref)
    out_ref[...] = filtered(total, mask_ref)


def update_kernel(ring_ref, mask_ref, rows_ref, own_ref, other_ref, tile_ref, out_ref):
    cube_term = own_ref[...] + ring_product(1 - ring_ref[0], rows_ref, other_ref)
    out_ref[...] = filtered(1.5 * tile_ref[...].astype(F32) - 0.5 * cube_term, mask_ref)


def copy_out(tile_ref, copies_ref, sem):
    made = [pltpu.make_async_copy(tile_ref, copies_ref.at[i], sem.at[i]) for i in range(copies_ref.shape[0])]
    for copy in made:
        copy.start()
    for copy in made:
        copy.wait()


def update_copies_kernel(
    ring_ref, mask_ref, rows_ref, own_ref, other_ref, tile_ref, out_ref, copies_ref, sem
):
    update_kernel(ring_ref, mask_ref, rows_ref, own_ref, other_ref, tile_ref, out_ref)
    copy_out(out_ref, copies_ref, sem)


SMEM = pl.BlockSpec(memory_space=pltpu.SMEM)
VMEM = pl.BlockSpec(memory_space=pltpu.VMEM)
ANY = pl.BlockSpec(memory_space=pl.ANY)


def call(kernel, scalars, arrays, out, copies=0):
    outs, specs, scratch = [out], [VMEM], []
    if copies:
        outs.append(jax.ShapeDtypeStruct((copies, *out.shape), out.dtype))
        specs.append(ANY)
        scratch.append(pltpu.SemaphoreType.DMA((copies,)))
    flops = sum(2 * a.size * out.shape[1] for a in arrays if a.ndim == 3)
    return pl.pallas_call(
        kernel,
        out_shape=outs,
        in_specs=[SMEM] * len(scalars) + [VMEM] * len(arrays),
        out_specs=specs,
        scratch_shapes=scratch,
        cost_estimate=pl.CostEstimate(
            flops=flops, bytes_accessed=sum(2 * a.size for a in arrays), transcendentals=0
        ),
        compiler_params=pltpu.CompilerParams(vmem_limit_bytes=32 << 20),
    )(*scalars, *arrays)


def broadcast(tile, copies):
    return pl.pallas_call(
        copy_out,
        out_shape=jax.ShapeDtypeStruct((copies, *tile.shape), tile.dtype),
        in_specs=[VMEM],
        out_specs=ANY,
        scratch_shapes=[pltpu.SemaphoreType.DMA((copies,))],
    )(tile)


def product(kernel, place, mask, rows, column, more, out, copies=0):
    chips = lax.axis_size("blk") // CORES
    rings = [[CORES * z + (z + p) % CORES for z in range(chips)] for p in range(CORES)]
    swap = [(CORES * z + k, CORES * z + 1 - k) for z in range(chips) for k in range(CORES)]
    ring = ((place // CORES + place) % CORES).astype(jnp.int32).reshape(1)
    own = lax.all_gather(column, "blk", axis=0, axis_index_groups=rings)
    other = lax.ppermute(own, "blk", swap)
    (half,) = call(own_kernel, [ring], [rows, own], jax.ShapeDtypeStruct(out.shape, F32))
    return call(kernel, [ring, mask], [rows, half, other, *more], out, copies)


def on_device(x_start, keep_mask):
    tiles = lax.axis_size(PLANE)
    place = lax.axis_index("blk")
    out = jax.ShapeDtypeStruct(x_start.shape, BF16)
    tile, copies = x_start, broadcast(x_start, tiles)
    for step in range(ITERS):
        rows = lax.all_to_all(copies, PLANE, 0, 0)
        (square,) = product(square_kernel, place, keep_mask[step, 0], rows, tile, [], out)
        if step < ITERS - 1:
            tile, copies = product(
                update_copies_kernel, place, keep_mask[step, 1], rows, square, [tile], out, tiles
            )
        else:
            (tile,) = product(update_kernel, place, keep_mask[step, 1], rows, square, [tile], out)
    return tile


def solution(mesh):
    spec = P("blk", PLANE)
    return jax.shard_map(
        on_device,
        mesh=mesh,
        in_specs=(spec, P(None, None, "blk", PLANE)),
        out_specs=spec,
        check_vma=False,
    )
```

```python
import functools

import jax
import jax.numpy as jnp
from jax import lax
from jax.experimental import pallas as pl
from jax.experimental.pallas import tpu as pltpu
from jax.sharding import PartitionSpec as P

BS = 64
ITERS = 2
CORES = 2
PLANE = ("row", "depth")
F32 = jnp.float32
BF16 = jnp.bfloat16


def ring_rows(ring, rows_ref):
    chips = rows_ref.shape[0] // CORES
    cores = [1 - ring if z % 2 else ring for z in range(chips)]
    return jnp.concatenate([rows_ref[CORES * z + cores[z]] for z in range(chips)], axis=1)


def times(left, column_ref):
    chips, side, cols = column_ref.shape
    return jnp.dot(left, column_ref[...].reshape(chips * side, cols), preferred_element_type=F32)


def expanded(mask_ref, shape):
    block_row = lax.broadcasted_iota(jnp.int32, shape, 0) // BS
    block_col = lax.broadcasted_iota(jnp.int32, shape, 1) // BS
    keep = jnp.zeros(shape, jnp.int32)
    for i in range(shape[0] // BS):
        for j in range(shape[1] // BS):
            here = jnp.logical_and(block_row == i, block_col == j)
            keep = jnp.where(here, mask_ref[i, j], keep)
    return keep


def own_kernel(scale, ring_ref, mask_ref, rows_ref, own_ref, *refs):
    *tile_ref, base_ref, left_ref, keep_ref = refs
    ring = ring_ref[0]
    base = scale * times(ring_rows(ring, rows_ref), own_ref)
    if tile_ref:
        base = 1.5 * tile_ref[0][...].astype(F32) + base
    base_ref[...] = base
    left_ref[...] = ring_rows(1 - ring, rows_ref)
    keep_ref[...] = expanded(mask_ref, keep_ref.shape)


def other_kernel(scale, base_ref, left_ref, keep_ref, other_ref, out_ref):
    total = base_ref[...] + scale * times(left_ref[...], other_ref)
    out_ref[...] = jnp.where(keep_ref[...] == 1, total, 0.0).astype(BF16)


def copy_out(tile, copies_ref, few_ref, sem):
    few = few_ref.shape[0]
    for i in range(few):
        few_ref[i] = tile
    made = [
        pltpu.make_async_copy(few_ref, copies_ref.at[pl.ds(few * i, few)], sem.at[i])
        for i in range(copies_ref.shape[0] // few)
    ]
    for copy in made:
        copy.start()
    for copy in made:
        copy.wait()


def other_copies_kernel(
    scale, base_ref, left_ref, keep_ref, other_ref, out_ref, copies_ref, few_ref, sem
):
    other_kernel(scale, base_ref, left_ref, keep_ref, other_ref, out_ref)
    copy_out(out_ref[...], copies_ref, few_ref, sem)


def broadcast_kernel(tile_ref, copies_ref, few_ref, sem):
    copy_out(tile_ref[...], copies_ref, few_ref, sem)


FEW = 4
SMEM = pl.BlockSpec(memory_space=pltpu.SMEM)
VMEM = pl.BlockSpec(memory_space=pltpu.VMEM)
ANY = pl.BlockSpec(memory_space=pl.ANY)


def call(kernel, scalars, arrays, outs, copies=0):
    specs, scratch = [VMEM] * len(outs), []
    if copies:
        shape = arrays[0].shape if not outs else outs[0].shape
        outs = [*outs, jax.ShapeDtypeStruct((copies, *shape), BF16)]
        specs.append(ANY)
        scratch = [pltpu.VMEM((FEW, *shape), BF16), pltpu.SemaphoreType.DMA((copies // FEW,))]
    work = sum(a.size for a in arrays)
    return pl.pallas_call(
        kernel,
        out_shape=outs,
        in_specs=[SMEM] * len(scalars) + [VMEM] * len(arrays),
        out_specs=specs,
        scratch_shapes=scratch,
        cost_estimate=pl.CostEstimate(
            flops=256 * work, bytes_accessed=2 * work, transcendentals=0
        ),
        compiler_params=pltpu.CompilerParams(vmem_limit_bytes=32 << 20),
    )(*scalars, *arrays)


def product(place, mask, rows, column, tile=None, copies=0):
    side, cols = column.shape
    chips = lax.axis_size("blk") // CORES
    rings = [[CORES * z + (z + p) % CORES for z in range(chips)] for p in range(CORES)]
    swap = [(CORES * z + k, CORES * z + 1 - k) for z in range(chips) for k in range(CORES)]
    ring = ((place // CORES + place) % CORES).astype(jnp.int32).reshape(1)
    own = lax.all_gather(column, "blk", axis=0, axis_index_groups=rings)
    other = lax.ppermute(own, "blk", swap)
    scale = 1.0 if tile is None else -0.5
    parts = call(
        functools.partial(own_kernel, scale),
        [ring, mask],
        [rows, own] + ([] if tile is None else [tile]),
        [
            jax.ShapeDtypeStruct((side, cols), F32),
            jax.ShapeDtypeStruct((side, chips * side), BF16),
            jax.ShapeDtypeStruct((side, cols), jnp.int32),
        ],
    )
    last = functools.partial(other_copies_kernel if copies else other_kernel, scale)
    return call(last, [], [*parts, other], [jax.ShapeDtypeStruct((side, cols), BF16)], copies)


def on_device(x_start, keep_mask):
    tiles = lax.axis_size(PLANE)
    place = lax.axis_index("blk")
    tile, (copies,) = x_start, call(broadcast_kernel, [], [x_start], [], tiles)
    for step in range(ITERS):
        rows = lax.all_to_all(copies, PLANE, 0, 0)
        (square,) = product(place, keep_mask[step, 0], rows, tile)
        more = tiles if step < ITERS - 1 else 0
        tile, *copies = product(place, keep_mask[step, 1], rows, square, tile, more)
        copies = copies[0] if copies else None
    return tile


def solution(mesh):
    spec = P("blk", PLANE)
    return jax.shard_map(
        on_device,
        mesh=mesh,
        in_specs=(spec, P(None, None, "blk", PLANE)),
        out_specs=spec,
        check_vma=False,
    )
```

```python
import functools

import jax
import jax.numpy as jnp
from jax import lax
from jax.experimental import pallas as pl
from jax.experimental.pallas import tpu as pltpu
from jax.sharding import PartitionSpec as P

BS = 64
ITERS = 2
CORES = 2
PLANE = ("row", "depth")
FEW = 4
F32 = jnp.float32
BF16 = jnp.bfloat16


def lanes(shape):
    return lax.broadcasted_iota(jnp.int32, shape, len(shape) - 1)


def pieces(values, place_ref):
    side = values[0].shape[0]
    half = side // 2
    ring, odd = place_ref[0:1, :] == 1, place_ref[1:2, :] == 1
    first = jnp.where(odd, values[1], values[0])
    second = jnp.where(odd, values[0], values[1])
    left = jnp.where(ring, pltpu.roll(first, half, 1), first)
    right = jnp.where(ring, second, pltpu.roll(second, half, 1))
    row_piece = jnp.where(lanes((side, side)) < half, left, right)
    column_piece = jnp.concatenate(
        [jnp.where(ring, value[half:], value[:half]) for value in values], axis=0
    )
    return row_piece.astype(BF16), column_piece.astype(BF16)


def copy_out(tile, copies_ref, few_ref, sem):
    few = few_ref.shape[0]
    for i in range(few):
        few_ref[i] = tile
    made = [
        pltpu.make_async_copy(few_ref, copies_ref.at[pl.ds(few * i, few)], sem.at[i])
        for i in range(copies_ref.shape[0] // few)
    ]
    for copy in made:
        copy.start()
    for copy in made:
        copy.wait()


def place_kernel(mask_ref, place_ref, entry_ref):
    width = entry_ref.shape[1]
    blk = lax.axis_index("blk")
    ring = (blk // CORES + blk) % CORES
    for i, value in enumerate((ring, lax.axis_index(PLANE) % CORES, blk % CORES)):
        place_ref[i : i + 1, :] = jnp.full((1, width), value, jnp.int32)
    row = 0
    for step in range(mask_ref.shape[0]):
        for which in range(mask_ref.shape[1]):
            for i in range(mask_ref.shape[2]):
                for j in range(mask_ref.shape[3]):
                    value = mask_ref[step, which, i, j].astype(F32)
                    entry_ref[row : row + 1, :] = jnp.full((1, width), value, F32)
                    row += 1


def first_kernel(both_ref, place_ref, column_ref, copies_ref, few_ref, sem):
    values = [both_ref[i].astype(F32) for i in range(CORES)]
    row_piece, column_piece = pieces(values, place_ref)
    column_ref[...] = column_piece
    copy_out(row_piece, copies_ref, few_ref, sem)


def partial_sums(rows_ref, columns_ref):
    chips, side, cols = columns_ref.shape
    half = side // 2
    low = lanes((side, side)) < half
    even = [rows_ref[CORES * z] for z in range(chips)]
    odd = [rows_ref[CORES * z + 1] for z in range(chips)]
    left0 = jnp.concatenate([jnp.where(low, e, o) for e, o in zip(even, odd)], axis=1)
    left1 = jnp.concatenate([jnp.where(low, o, e) for e, o in zip(even, odd)], axis=1)
    right0 = columns_ref[...].reshape(chips * side, cols)
    right1 = jnp.concatenate(
        [columns_ref[z, h * half : (h + 1) * half] for z in range(chips) for h in (1, 0)], axis=0
    )
    return [
        jnp.dot(left, right, preferred_element_type=F32)
        for left, right in ((left0, right0), (left1, right1))
    ]


def partial_kernel(rows_ref, columns_ref, *refs):
    *entry_ref, out_ref = refs
    side = columns_ref.shape[1]
    for i, value in enumerate(partial_sums(rows_ref, columns_ref)):
        out_ref[i * side : (i + 1) * side, :] = value
    if entry_ref:
        out_ref[CORES * side :, :] = entry_ref[0][...]


def filtered(value, entries, number):
    side = value.shape[0]
    each = side // BS
    low = lanes((1, value.shape[1])) < BS
    rows = []
    for i in range(each):
        at = (number * each + i) * each
        rows.append(jnp.where(low, entries[at : at + 1, :], entries[at + 1 : at + 2, :]))
    block_row = lax.broadcasted_iota(jnp.int32, value.shape, 0) // BS
    keep = jnp.where(block_row == 0, rows[0], rows[1])
    return jnp.where(keep == 1.0, value, 0.0).astype(BF16).astype(F32)


def square_kernel(first, number, sums_ref, *refs):
    if first:
        place_ref, column_ref, entries_ref = refs
        side = column_ref.shape[0]
        for i in range(CORES):
            entries_ref[i] = sums_ref[i, CORES * side :, :]
    else:
        place_ref, entries_ref, column_ref = refs
        side = column_ref.shape[0]
    values = []
    for i in range(CORES):
        at = slice(i * side, (i + 1) * side)
        values.append(filtered(sums_ref[0, at, :] + sums_ref[1, at, :], entries_ref[i], number))
    column_ref[...] = pieces(values, place_ref)[1]


def updated(number, sums_ref, entries_ref, both_ref):
    side = both_ref.shape[1]
    values = []
    for i in range(CORES):
        at = slice(i * side, (i + 1) * side)
        cube_term = sums_ref[0, at, :] + sums_ref[1, at, :]
        value = 1.5 * both_ref[i].astype(F32) - 0.5 * cube_term
        values.append(filtered(value, entries_ref[i], number))
    return values


def update_kernel(
    number, sums_ref, place_ref, entries_ref, both_ref, new_ref, column_ref, copies_ref, few_ref, sem
):
    values = updated(number, sums_ref, entries_ref, both_ref)
    for i in range(CORES):
        new_ref[i] = values[i].astype(BF16)
    row_piece, column_piece = pieces(values, place_ref)
    column_ref[...] = column_piece
    copy_out(row_piece, copies_ref, few_ref, sem)


def last_kernel(number, sums_ref, place_ref, entries_ref, both_ref, out_ref):
    values = updated(number, sums_ref, entries_ref, both_ref)
    out_ref[...] = jnp.where(place_ref[2:3, :] == 1, values[1], values[0]).astype(BF16)


def call(kernel, scalars, arrays, outs, copies=None):
    specs, scratch = [pl.BlockSpec(memory_space=pltpu.VMEM)] * len(outs), []
    if copies is not None:
        outs = [*outs, copies]
        specs.append(pl.BlockSpec(memory_space=pl.ANY))
        few, number = (FEW, *copies.shape[1:]), copies.shape[0] // FEW
        scratch = [pltpu.VMEM(few, copies.dtype), pltpu.SemaphoreType.DMA((number,))]
    work = sum(a.size for a in arrays)
    return pl.pallas_call(
        kernel,
        out_shape=outs,
        in_specs=[pl.BlockSpec(memory_space=pltpu.SMEM)] * len(scalars)
        + [pl.BlockSpec(memory_space=pltpu.VMEM)] * len(arrays),
        out_specs=specs,
        scratch_shapes=scratch,
        cost_estimate=pl.CostEstimate(
            flops=256 * work, bytes_accessed=2 * work, transcendentals=0
        ),
        compiler_params=pltpu.CompilerParams(vmem_limit_bytes=32 << 20),
    )(*scalars, *arrays)


def on_device(x_start, keep_mask):
    side, cols = x_start.shape
    tiles = lax.axis_size(PLANE)
    chips = lax.axis_size("blk") // CORES
    rings = [[CORES * z + (z + p) % CORES for z in range(chips)] for p in range(CORES)]
    pairs = [[CORES * z + k for k in range(CORES)] for z in range(chips)]

    shape = jax.ShapeDtypeStruct
    tile = shape((side, cols), BF16)
    two_tiles = shape((CORES, side, cols), BF16)
    copied = shape((tiles, side, cols), BF16)
    entry = shape((keep_mask.size, cols), F32)

    def between_cores(value):
        return lax.all_gather(value, "blk", axis=0, axis_index_groups=pairs)

    def summed(rows, column, more=()):
        columns = lax.all_gather(column, "blk", axis=0, axis_index_groups=rings)
        height = CORES * side + sum(a.shape[0] for a in more)
        (partial,) = call(partial_kernel, [], [rows, columns, *more], [shape((height, cols), F32)])
        return between_cores(partial)

    place, entries = call(place_kernel, [keep_mask], [], [shape((8, cols), jnp.int32), entry])
    place, entries, x_start = lax.optimization_barrier((place, entries, x_start))
    both = between_cores(x_start)
    column, copies = call(first_kernel, [], [both, place], [tile], copied)
    for step in range(ITERS):
        first, last = step == 0, step == ITERS - 1
        rows = lax.all_to_all(copies, PLANE, 0, 0)
        sums = summed(rows, column, [entries] if first else [])
        square = functools.partial(square_kernel, first, 2 * step)
        if first:
            outs = [tile, shape((CORES, *entry.shape), F32)]
            column, entries = call(square, [], [sums, place], outs)
        else:
            (column,) = call(square, [], [sums, place, entries], [tile])
        given = [summed(rows, column), place, entries, both]
        if last:
            (out,) = call(functools.partial(last_kernel, 2 * step + 1), [], given, [tile])
        else:
            update = functools.partial(update_kernel, 2 * step + 1)
            both, column, copies = call(update, [], given, [two_tiles, tile], copied)
    return out


def solution(mesh):
    spec = P("blk", PLANE)
    return jax.shard_map(
        on_device,
        mesh=mesh,
        in_specs=(spec, P(None, None, "blk", PLANE)),
        out_specs=spec,
        check_vma=False,
    )
```

```python
import functools

import jax
import jax.numpy as jnp
from jax import lax
from jax.experimental import pallas as pl
from jax.experimental.pallas import tpu as pltpu
from jax.sharding import PartitionSpec as P

BS = 64
ITERS = 2
CORES = 2
PLANE = ("row", "depth")
FEW = 4
F32 = jnp.float32
BF16 = jnp.bfloat16


def lanes(shape):
    return lax.broadcasted_iota(jnp.int32, shape, len(shape) - 1)


def pieces(values):
    side = values[0].shape[0]
    half = side // 2
    blk = lax.axis_index("blk")
    ring = jnp.full((1, side), (blk // CORES + blk) % CORES, jnp.int32) == 1
    odd = jnp.full((1, side), lax.axis_index(PLANE) % CORES, jnp.int32) == 1
    first = jnp.where(odd, values[1], values[0])
    second = jnp.where(odd, values[0], values[1])
    left = jnp.where(ring, pltpu.roll(first, half, 1), first)
    right = jnp.where(ring, second, pltpu.roll(second, half, 1))
    row_piece = jnp.where(lanes((side, side)) < half, left, right)
    column_piece = jnp.concatenate(
        [jnp.where(ring, value[half:], value[:half]) for value in values], axis=0
    )
    return row_piece.astype(BF16), column_piece.astype(BF16)


def copy_out(tile, copies_ref, few_ref, sem):
    few = few_ref.shape[0]
    for i in range(few):
        few_ref[i] = tile
    made = [
        pltpu.make_async_copy(few_ref, copies_ref.at[pl.ds(few * i, few)], sem.at[i])
        for i in range(copies_ref.shape[0] // few)
    ]
    for copy in made:
        copy.start()
    for copy in made:
        copy.wait()


def first_kernel(both_ref, column_ref, copies_ref, few_ref, sem):
    values = [both_ref[i].astype(F32) for i in range(CORES)]
    row_piece, column_piece = pieces(values)
    column_ref[...] = column_piece
    copy_out(row_piece, copies_ref, few_ref, sem)


def partial_sums(rows_ref, columns_ref):
    chips, side, cols = columns_ref.shape
    half = side // 2
    low = lanes((side, side)) < half
    even = [rows_ref[CORES * z] for z in range(chips)]
    odd = [rows_ref[CORES * z + 1] for z in range(chips)]
    left0 = jnp.concatenate([jnp.where(low, e, o) for e, o in zip(even, odd)], axis=1)
    left1 = jnp.concatenate([jnp.where(low, o, e) for e, o in zip(even, odd)], axis=1)
    right0 = columns_ref[...].reshape(chips * side, cols)
    right1 = jnp.concatenate(
        [columns_ref[z, h * half : (h + 1) * half] for z in range(chips) for h in (1, 0)], axis=0
    )
    return [
        jnp.dot(left, right, preferred_element_type=F32)
        for left, right in ((left0, right0), (left1, right1))
    ]


def partial_kernel(rows_ref, columns_ref, *refs):
    *entry_ref, out_ref = refs
    side = columns_ref.shape[1]
    for i, value in enumerate(partial_sums(rows_ref, columns_ref)):
        out_ref[i * side : (i + 1) * side, :] = value
    if entry_ref:
        out_ref[CORES * side :, :] = entry_ref[0][...]


def filtered(value, entries, number):
    side = value.shape[0]
    each = side // BS
    low = lanes((1, value.shape[1])) < BS
    rows = []
    for i in range(each):
        at = (number * each + i) * each
        rows.append(jnp.where(low, entries[at : at + 1, :], entries[at + 1 : at + 2, :]))
    block_row = lax.broadcasted_iota(jnp.int32, value.shape, 0) // BS
    keep = jnp.where(block_row == 0, rows[0], rows[1])
    return jnp.where(keep == 1.0, value, 0.0).astype(BF16).astype(F32)


def square_kernel(first, number, sums_ref, *refs):
    if first:
        column_ref, entries_ref = refs
        side = column_ref.shape[0]
        for i in range(CORES):
            entries_ref[i] = sums_ref[i, CORES * side :, :]
    else:
        entries_ref, column_ref = refs
        side = column_ref.shape[0]
    values = []
    for i in range(CORES):
        at = slice(i * side, (i + 1) * side)
        values.append(filtered(sums_ref[0, at, :] + sums_ref[1, at, :], entries_ref[i], number))
    column_ref[...] = pieces(values)[1]


def updated(number, sums_ref, entries_ref, both_ref):
    side = both_ref.shape[1]
    values = []
    for i in range(CORES):
        at = slice(i * side, (i + 1) * side)
        cube_term = sums_ref[0, at, :] + sums_ref[1, at, :]
        value = 1.5 * both_ref[i].astype(F32) - 0.5 * cube_term
        values.append(filtered(value, entries_ref[i], number))
    return values


def update_kernel(
    number, sums_ref, entries_ref, both_ref, new_ref, column_ref, copies_ref, few_ref, sem
):
    values = updated(number, sums_ref, entries_ref, both_ref)
    for i in range(CORES):
        new_ref[i] = values[i].astype(BF16)
    row_piece, column_piece = pieces(values)
    column_ref[...] = column_piece
    copy_out(row_piece, copies_ref, few_ref, sem)


def last_kernel(number, sums_ref, entries_ref, both_ref, out_ref):
    values = updated(number, sums_ref, entries_ref, both_ref)
    core = jnp.full((1, out_ref.shape[1]), lax.axis_index("blk") % CORES, jnp.int32)
    out_ref[...] = jnp.where(core == 1, values[1], values[0]).astype(BF16)


def call(kernel, scalars, arrays, outs, copies=None):
    specs, scratch = [pl.BlockSpec(memory_space=pltpu.VMEM)] * len(outs), []
    if copies is not None:
        outs = [*outs, copies]
        specs.append(pl.BlockSpec(memory_space=pl.ANY))
        few, number = (FEW, *copies.shape[1:]), copies.shape[0] // FEW
        scratch = [pltpu.VMEM(few, copies.dtype), pltpu.SemaphoreType.DMA((number,))]
    work = sum(a.size for a in arrays)
    return pl.pallas_call(
        kernel,
        out_shape=outs,
        in_specs=[pl.BlockSpec(memory_space=pltpu.SMEM)] * len(scalars)
        + [pl.BlockSpec(memory_space=pltpu.VMEM)] * len(arrays),
        out_specs=specs,
        scratch_shapes=scratch,
        cost_estimate=pl.CostEstimate(
            flops=256 * work, bytes_accessed=2 * work, transcendentals=0
        ),
        compiler_params=pltpu.CompilerParams(vmem_limit_bytes=32 << 20),
    )(*scalars, *arrays)


def on_device(x_start, keep_mask):
    side, cols = x_start.shape
    tiles = lax.axis_size(PLANE)
    chips = lax.axis_size("blk") // CORES
    rings = [[CORES * z + (z + p) % CORES for z in range(chips)] for p in range(CORES)]
    pairs = [[CORES * z + k for k in range(CORES)] for z in range(chips)]

    shape = jax.ShapeDtypeStruct
    tile = shape((side, cols), BF16)
    two_tiles = shape((CORES, side, cols), BF16)
    copied = shape((tiles, side, cols), BF16)
    entry = shape((keep_mask.size, cols), F32)

    def between_cores(value):
        return lax.all_gather(value, "blk", axis=0, axis_index_groups=pairs)

    def summed(rows, column, more=()):
        columns = lax.all_gather(column, "blk", axis=0, axis_index_groups=rings)
        height = CORES * side + sum(a.shape[0] for a in more)
        (partial,) = call(partial_kernel, [], [rows, columns, *more], [shape((height, cols), F32)])
        return between_cores(partial)

    entries = jnp.broadcast_to(keep_mask.reshape(-1, 1), entry.shape).astype(F32)
    entries, x_start = lax.optimization_barrier((entries, x_start))
    both = between_cores(x_start)
    column, copies = call(first_kernel, [], [both], [tile], copied)
    for step in range(ITERS):
        first, last = step == 0, step == ITERS - 1
        rows = lax.all_to_all(copies, PLANE, 0, 0)
        sums = summed(rows, column, [entries] if first else [])
        square = functools.partial(square_kernel, first, 2 * step)
        if first:
            outs = [tile, shape((CORES, *entry.shape), F32)]
            column, entries = call(square, [], [sums], outs)
        else:
            (column,) = call(square, [], [sums, entries], [tile])
        given = [summed(rows, column), entries, both]
        if last:
            (out,) = call(functools.partial(last_kernel, 2 * step + 1), [], given, [tile])
        else:
            update = functools.partial(update_kernel, 2 * step + 1)
            both, column, copies = call(update, [], given, [two_tiles, tile], copied)
    return out


def solution(mesh):
    spec = P("blk", PLANE)
    return jax.shard_map(
        on_device,
        mesh=mesh,
        in_specs=(spec, P(None, None, "blk", PLANE)),
        out_specs=spec,
        check_vma=False,
    )
```

```python
import functools

import jax
import jax.numpy as jnp
from jax import lax
from jax.experimental import pallas as pl
from jax.experimental.pallas import tpu as pltpu
from jax.sharding import PartitionSpec as P

BS = 64
ITERS = 2
CORES = 2
PLANE = ("row", "depth")
FEW = 4
F32 = jnp.float32
BF16 = jnp.bfloat16


def lanes(shape):
    return lax.broadcasted_iota(jnp.int32, shape, len(shape) - 1)


def pieces(values):
    side = values[0].shape[0]
    half = side // 2
    blk = lax.axis_index("blk")
    ring = jnp.full((1, side), (blk // CORES + blk) % CORES, jnp.int32) == 1
    odd = jnp.full((1, side), lax.axis_index(PLANE) % CORES, jnp.int32) == 1
    first = jnp.where(odd, values[1], values[0])
    second = jnp.where(odd, values[0], values[1])
    left = jnp.where(ring, pltpu.roll(first, half, 1), first)
    right = jnp.where(ring, second, pltpu.roll(second, half, 1))
    row_piece = jnp.where(lanes((side, side)) < half, left, right)
    column_piece = jnp.concatenate(
        [jnp.where(ring, value[half:], value[:half]) for value in values], axis=0
    )
    return row_piece.astype(BF16), column_piece.astype(BF16)


def copy_out(tile, copies_ref, few_ref, sem):
    few = few_ref.shape[0]
    for i in range(few):
        few_ref[i] = tile
    made = [
        pltpu.make_async_copy(few_ref, copies_ref.at[pl.ds(few * i, few)], sem.at[i])
        for i in range(copies_ref.shape[0] // few)
    ]
    for copy in made:
        copy.start()
    for copy in made:
        copy.wait()


def first_kernel(both_ref, column_ref, copies_ref, few_ref, sem):
    values = [both_ref[i].astype(F32) for i in range(CORES)]
    row_piece, column_piece = pieces(values)
    column_ref[...] = column_piece
    copy_out(row_piece, copies_ref, few_ref, sem)


def partial_sums(rows_ref, columns_ref):
    chips, side, cols = columns_ref.shape
    half = side // 2
    low = lanes((side, side)) < half
    even = [rows_ref[CORES * z] for z in range(chips)]
    odd = [rows_ref[CORES * z + 1] for z in range(chips)]
    left0 = jnp.concatenate([jnp.where(low, e, o) for e, o in zip(even, odd)], axis=1)
    left1 = jnp.concatenate([jnp.where(low, o, e) for e, o in zip(even, odd)], axis=1)
    right0 = columns_ref[...].reshape(chips * side, cols)
    right1 = jnp.concatenate(
        [columns_ref[z, h * half : (h + 1) * half] for z in range(chips) for h in (1, 0)], axis=0
    )
    return [
        jnp.dot(left, right, preferred_element_type=F32)
        for left, right in ((left0, right0), (left1, right1))
    ]


def partial_kernel(rows_ref, columns_ref, *refs):
    *entry_ref, out_ref = refs
    side = columns_ref.shape[1]
    for i, value in enumerate(partial_sums(rows_ref, columns_ref)):
        out_ref[i * side : (i + 1) * side, :] = value
    if entry_ref:
        out_ref[CORES * side :, :] = entry_ref[0][...]


def filtered(value, entries, number):
    side = value.shape[0]
    each = side // BS
    low = lanes((1, value.shape[1])) < BS
    rows = []
    for i in range(each):
        at = (number * each + i) * each
        rows.append(jnp.where(low, entries[at : at + 1, :], entries[at + 1 : at + 2, :]))
    block_row = lax.broadcasted_iota(jnp.int32, value.shape, 0) // BS
    keep = jnp.where(block_row == 0, rows[0], rows[1])
    return jnp.where(keep == 1.0, value, 0.0).astype(BF16).astype(F32)


def square_kernel(first, number, sums_ref, *refs):
    if first:
        column_ref, entries_ref = refs
        side = column_ref.shape[0]
        for i in range(CORES):
            entries_ref[i] = sums_ref[i, CORES * side :, :]
    else:
        entries_ref, column_ref = refs
        side = column_ref.shape[0]
    values = []
    for i in range(CORES):
        at = slice(i * side, (i + 1) * side)
        values.append(filtered(sums_ref[0, at, :] + sums_ref[1, at, :], entries_ref[i], number))
    column_ref[...] = pieces(values)[1]


def updated(number, sums_ref, entries_ref, both_ref):
    side = both_ref.shape[1]
    values = []
    for i in range(CORES):
        at = slice(i * side, (i + 1) * side)
        cube_term = sums_ref[0, at, :] + sums_ref[1, at, :]
        value = 1.5 * both_ref[i].astype(F32) - 0.5 * cube_term
        values.append(filtered(value, entries_ref[i], number))
    return values


def update_kernel(
    number, sums_ref, entries_ref, both_ref, new_ref, column_ref, copies_ref, few_ref, sem
):
    values = updated(number, sums_ref, entries_ref, both_ref)
    for i in range(CORES):
        new_ref[i] = values[i].astype(BF16)
    row_piece, column_piece = pieces(values)
    column_ref[...] = column_piece
    copy_out(row_piece, copies_ref, few_ref, sem)


def last_partial_kernel(rows_ref, columns_ref, sent_ref, kept_ref):
    value = partial_sums(rows_ref, columns_ref)
    core = jnp.full((1, sent_ref.shape[1]), lax.axis_index("blk") % CORES, jnp.int32) == 1
    sent_ref[...] = jnp.where(core, value[0], value[1])
    kept_ref[...] = jnp.where(core, value[1], value[0])


def last_kernel(number, sent_ref, kept_ref, entries_ref, both_ref, out_ref):
    core = lax.axis_index("blk") % CORES
    cube_term = kept_ref[...] + sent_ref[1 - core]
    value = 1.5 * both_ref[core].astype(F32) - 0.5 * cube_term
    out_ref[...] = filtered(value, entries_ref[core], number).astype(BF16)


def call(kernel, scalars, arrays, outs, copies=None):
    specs, scratch = [pl.BlockSpec(memory_space=pltpu.VMEM)] * len(outs), []
    if copies is not None:
        outs = [*outs, copies]
        specs.append(pl.BlockSpec(memory_space=pl.ANY))
        few, number = (FEW, *copies.shape[1:]), copies.shape[0] // FEW
        scratch = [pltpu.VMEM(few, copies.dtype), pltpu.SemaphoreType.DMA((number,))]
    work = sum(a.size for a in arrays)
    return pl.pallas_call(
        kernel,
        out_shape=outs,
        in_specs=[pl.BlockSpec(memory_space=pltpu.SMEM)] * len(scalars)
        + [pl.BlockSpec(memory_space=pltpu.VMEM)] * len(arrays),
        out_specs=specs,
        scratch_shapes=scratch,
        cost_estimate=pl.CostEstimate(
            flops=256 * work, bytes_accessed=2 * work, transcendentals=0
        ),
        compiler_params=pltpu.CompilerParams(vmem_limit_bytes=32 << 20),
    )(*scalars, *arrays)


def on_device(x_start, keep_mask):
    side, cols = x_start.shape
    tiles = lax.axis_size(PLANE)
    chips = lax.axis_size("blk") // CORES
    rings = [[CORES * z + (z + p) % CORES for z in range(chips)] for p in range(CORES)]
    pairs = [[CORES * z + k for k in range(CORES)] for z in range(chips)]

    shape = jax.ShapeDtypeStruct
    tile = shape((side, cols), BF16)
    two_tiles = shape((CORES, side, cols), BF16)
    copied = shape((tiles, side, cols), BF16)
    entry = shape((keep_mask.size, cols), F32)

    def between_cores(value):
        return lax.all_gather(value, "blk", axis=0, axis_index_groups=pairs)

    def summed(rows, column, more=()):
        columns = lax.all_gather(column, "blk", axis=0, axis_index_groups=rings)
        height = CORES * side + sum(a.shape[0] for a in more)
        (partial,) = call(partial_kernel, [], [rows, columns, *more], [shape((height, cols), F32)])
        return between_cores(partial)

    entries = jnp.broadcast_to(keep_mask.reshape(-1, 1), entry.shape).astype(F32)
    entries, x_start = lax.optimization_barrier((entries, x_start))
    both = between_cores(x_start)
    column, copies = call(first_kernel, [], [both], [tile], copied)
    for step in range(ITERS):
        first, last = step == 0, step == ITERS - 1
        rows = lax.all_to_all(copies, PLANE, 0, 0)
        sums = summed(rows, column, [entries] if first else [])
        square = functools.partial(square_kernel, first, 2 * step)
        if first:
            outs = [tile, shape((CORES, *entry.shape), F32)]
            column, entries = call(square, [], [sums], outs)
        else:
            (column,) = call(square, [], [sums, entries], [tile])
        if last:
            columns = lax.all_gather(column, "blk", axis=0, axis_index_groups=rings)
            sums = [shape((side, cols), F32)] * CORES
            sent, kept = call(last_partial_kernel, [], [rows, columns], sums)
            given = [between_cores(sent), kept, entries, both]
            (out,) = call(functools.partial(last_kernel, 2 * step + 1), [], given, [tile])
        else:
            given = [summed(rows, column), entries, both]
            update = functools.partial(update_kernel, 2 * step + 1)
            both, column, copies = call(update, [], given, [two_tiles, tile], copied)
    return out


def solution(mesh):
    spec = P("blk", PLANE)
    return jax.shard_map(
        on_device,
        mesh=mesh,
        in_specs=(spec, P(None, None, "blk", PLANE)),
        out_specs=spec,
        check_vma=False,
    )
```

```python
import functools

import jax
import jax.numpy as jnp
from jax import lax
from jax.experimental import pallas as pl
from jax.experimental.pallas import tpu as pltpu
from jax.sharding import PartitionSpec as P

BS = 64
ITERS = 2
CORES = 2
PLANE = ("row", "depth")
FEW = 4
F32 = jnp.float32
BF16 = jnp.bfloat16


def lanes(shape):
    return lax.broadcasted_iota(jnp.int32, shape, len(shape) - 1)


def pieces(values):
    side = values[0].shape[0]
    half = side // 2
    blk = lax.axis_index("blk")
    ring = jnp.full((1, side), (blk // CORES + blk) % CORES, jnp.int32) == 1
    odd = jnp.full((1, side), lax.axis_index(PLANE) % CORES, jnp.int32) == 1
    first = jnp.where(odd, values[1], values[0])
    second = jnp.where(odd, values[0], values[1])
    left = jnp.where(ring, pltpu.roll(first, half, 1), first)
    right = jnp.where(ring, second, pltpu.roll(second, half, 1))
    row_piece = jnp.where(lanes((side, side)) < half, left, right)
    column_piece = jnp.concatenate(
        [jnp.where(ring, value[half:], value[:half]) for value in values], axis=0
    )
    return row_piece.astype(BF16), column_piece.astype(BF16)


def copy_out(tile, copies_ref, few_ref, sem):
    few = few_ref.shape[0]
    for i in range(few):
        few_ref[i] = tile
    made = [
        pltpu.make_async_copy(few_ref, copies_ref.at[pl.ds(few * i, few)], sem.at[i])
        for i in range(copies_ref.shape[0] // few)
    ]
    for copy in made:
        copy.start()
    for copy in made:
        copy.wait()


def first_kernel(both_ref, column_ref, copies_ref, few_ref, sem):
    values = [both_ref[i].astype(F32) for i in range(CORES)]
    row_piece, column_piece = pieces(values)
    column_ref[...] = column_piece
    copy_out(row_piece, copies_ref, few_ref, sem)


def partial_sums(rows_ref, columns_ref):
    chips, side, cols = columns_ref.shape
    half = side // 2
    low = lanes((side, side)) < half
    even = [rows_ref[CORES * z] for z in range(chips)]
    odd = [rows_ref[CORES * z + 1] for z in range(chips)]
    left0 = jnp.concatenate([jnp.where(low, e, o) for e, o in zip(even, odd)], axis=1)
    left1 = jnp.concatenate([jnp.where(low, o, e) for e, o in zip(even, odd)], axis=1)
    right0 = columns_ref[...].reshape(chips * side, cols)
    right1 = jnp.concatenate(
        [columns_ref[z, h * half : (h + 1) * half] for z in range(chips) for h in (1, 0)], axis=0
    )
    return [
        jnp.dot(left, right, preferred_element_type=F32)
        for left, right in ((left0, right0), (left1, right1))
    ]


def partial_kernel(rows_ref, columns_ref, *refs):
    *entry_ref, out_ref = refs
    side = columns_ref.shape[1]
    for i, value in enumerate(partial_sums(rows_ref, columns_ref)):
        out_ref[i * side : (i + 1) * side, :] = value
    if entry_ref:
        out_ref[CORES * side :, :] = entry_ref[0][...]


def filtered(value, entries, number):
    side = value.shape[0]
    each = side // BS
    low = lanes((1, value.shape[1])) < BS
    rows = []
    for i in range(each):
        at = (number * each + i) * each
        rows.append(jnp.where(low, entries[at : at + 1, :], entries[at + 1 : at + 2, :]))
    block_row = lax.broadcasted_iota(jnp.int32, value.shape, 0) // BS
    keep = jnp.where(block_row == 0, rows[0], rows[1])
    return jnp.where(keep == 1.0, value, 0.0).astype(BF16).astype(F32)


def square_kernel(first, number, sums_ref, *refs):
    if first:
        column_ref, entries_ref = refs
        side = column_ref.shape[0]
        for i in range(CORES):
            entries_ref[i] = sums_ref[i, CORES * side :, :]
    else:
        entries_ref, column_ref = refs
        side = column_ref.shape[0]
    half = side // 2
    blk = lax.axis_index("blk")
    ring = (blk // CORES + blk) % CORES
    low = lanes((1, column_ref.shape[1])) < BS
    upper = jnp.full((1, column_ref.shape[1]), ring, jnp.int32) == 1
    each = side // BS
    for i in range(CORES):
        at = pl.ds(pl.multiple_of(i * side + ring * half, half), half)
        value = sums_ref[0, at, :] + sums_ref[1, at, :]
        rows = []
        for j in range(each):
            row = (number * each + j) * each
            left, right = entries_ref[i, row : row + 1, :], entries_ref[i, row + 1 : row + 2, :]
            rows.append(jnp.where(low, left, right))
        keep = jnp.where(upper, rows[1], rows[0])
        value = jnp.where(keep == 1.0, value, 0.0)
        column_ref[i * half : (i + 1) * half, :] = value.astype(BF16)


def updated(number, sums_ref, entries_ref, both_ref):
    side = both_ref.shape[1]
    values = []
    for i in range(CORES):
        at = slice(i * side, (i + 1) * side)
        cube_term = sums_ref[0, at, :] + sums_ref[1, at, :]
        value = 1.5 * both_ref[i].astype(F32) - 0.5 * cube_term
        values.append(filtered(value, entries_ref[i], number))
    return values


def update_kernel(
    number, sums_ref, entries_ref, both_ref, new_ref, column_ref, copies_ref, few_ref, sem
):
    values = updated(number, sums_ref, entries_ref, both_ref)
    for i in range(CORES):
        new_ref[i] = values[i].astype(BF16)
    row_piece, column_piece = pieces(values)
    column_ref[...] = column_piece
    copy_out(row_piece, copies_ref, few_ref, sem)


def last_kernel(number, sums_ref, entries_ref, both_ref, out_ref):
    values = updated(number, sums_ref, entries_ref, both_ref)
    core = jnp.full((1, out_ref.shape[1]), lax.axis_index("blk") % CORES, jnp.int32)
    out_ref[...] = jnp.where(core == 1, values[1], values[0]).astype(BF16)


def call(kernel, scalars, arrays, outs, copies=None):
    specs, scratch = [pl.BlockSpec(memory_space=pltpu.VMEM)] * len(outs), []
    if copies is not None:
        outs = [*outs, copies]
        specs.append(pl.BlockSpec(memory_space=pl.ANY))
        few, number = (FEW, *copies.shape[1:]), copies.shape[0] // FEW
        scratch = [pltpu.VMEM(few, copies.dtype), pltpu.SemaphoreType.DMA((number,))]
    work = sum(a.size for a in arrays)
    return pl.pallas_call(
        kernel,
        out_shape=outs,
        in_specs=[pl.BlockSpec(memory_space=pltpu.SMEM)] * len(scalars)
        + [pl.BlockSpec(memory_space=pltpu.VMEM)] * len(arrays),
        out_specs=specs,
        scratch_shapes=scratch,
        cost_estimate=pl.CostEstimate(
            flops=256 * work, bytes_accessed=2 * work, transcendentals=0
        ),
        compiler_params=pltpu.CompilerParams(vmem_limit_bytes=32 << 20),
    )(*scalars, *arrays)


def on_device(x_start, keep_mask):
    side, cols = x_start.shape
    tiles = lax.axis_size(PLANE)
    chips = lax.axis_size("blk") // CORES
    rings = [[CORES * z + (z + p) % CORES for z in range(chips)] for p in range(CORES)]
    pairs = [[CORES * z + k for k in range(CORES)] for z in range(chips)]

    shape = jax.ShapeDtypeStruct
    tile = shape((side, cols), BF16)
    two_tiles = shape((CORES, side, cols), BF16)
    copied = shape((tiles, side, cols), BF16)
    entry = shape((keep_mask.size, cols), F32)

    def between_cores(value):
        return lax.all_gather(value, "blk", axis=0, axis_index_groups=pairs)

    def summed(rows, column, more=()):
        columns = lax.all_gather(column, "blk", axis=0, axis_index_groups=rings)
        height = CORES * side + sum(a.shape[0] for a in more)
        (partial,) = call(partial_kernel, [], [rows, columns, *more], [shape((height, cols), F32)])
        return between_cores(partial)

    entries = jnp.broadcast_to(keep_mask.reshape(-1, 1), entry.shape).astype(F32)
    entries, x_start = lax.optimization_barrier((entries, x_start))
    both = between_cores(x_start)
    column, copies = call(first_kernel, [], [both], [tile], copied)
    for step in range(ITERS):
        first, last = step == 0, step == ITERS - 1
        rows = lax.all_to_all(copies, PLANE, 0, 0)
        sums = summed(rows, column, [entries] if first else [])
        square = functools.partial(square_kernel, first, 2 * step)
        if first:
            outs = [tile, shape((CORES, *entry.shape), F32)]
            column, entries = call(square, [], [sums], outs)
        else:
            (column,) = call(square, [], [sums, entries], [tile])
        given = [summed(rows, column), entries, both]
        if last:
            (out,) = call(functools.partial(last_kernel, 2 * step + 1), [], given, [tile])
        else:
            update = functools.partial(update_kernel, 2 * step + 1)
            both, column, copies = call(update, [], given, [two_tiles, tile], copied)
    return out


def solution(mesh):
    spec = P("blk", PLANE)
    return jax.shard_map(
        on_device,
        mesh=mesh,
        in_specs=(spec, P(None, None, "blk", PLANE)),
        out_specs=spec,
        check_vma=False,
    )
```
